512 devices in a mesh: row: 32 (over x, z), col: 16 (over y, core).
Axes of the slice: x: 4, y: 8, z: 8, core: 2. Of those that a mesh axis runs over, the one named last changes fastest.
Arguments:
- eigvectors: bfloat16 [98304, 2048], P('row', 'col'), may hold values from -0.4375 to 0.4375
- panel_vectors: bfloat16 [2, 256, 98304], P(None, 'col', 'row'), may hold values from -0.21875 to 0.21875
- panel_factors: float32 [2, 256, 256], replicated, may hold values from -0.375 to 0.375
- eigenvalues: float32 [2048], replicated, may hold values from 4 to 400
- damping: float32 [2048], replicated, may hold values from 0.02 to 0.1
- frequencies: float32 [8], replicated, may hold values from 4 to 16
- loads: bfloat16 [64, 98304], P(None, ('row', 'col')), may hold values from -6 to 6
Outputs:
- resp_real: bfloat16 [8, 64, 98304], P(None, None, ('row', 'col'))
- resp_imag: bfloat16 [8, 64, 98304], P(None, None, ('row', 'col'))
The draws below stay inside these ranges and needn't reach their ends.
All inputs are finite; a program needn't handle non-finite values.
Results may differ from the reference program's by a relative error of at most 0.015.
Values may be sent and summed in bfloat16 or wider, within the bound.
No kernel may reach another device: no remote copies, remote signals or barrier semaphores. Data moves between devices by JAX's collectives and lax.ppermute only.
A program may use at most 64 MiB of HBM per device.

```python
import math
import jax
import jax.numpy as jnp
from jax import lax

N = 98304
M = 2048
P_SIZE = 256
L = 64
FREQ = 8


def shard_levels(stream_key, dims, shards, low, high):
    def one(axis_at, parts):
        steps = jax.random.uniform(jax.random.fold_in(jax.random.fold_in(stream_key, 6), axis_at), (parts,), jnp.float32, low / len(shards), high / len(shards))
        return jnp.repeat(jnp.exp(steps), dims[axis_at] // parts).reshape((-1,) + (1,) * (len(dims) - axis_at - 1))

    level = one(*shards[0])
    for cut in shards[1:]:
        level = level * one(*cut)
    return level


def normal_values(stream_key, extent, scale, bound, split=(), held_as=jnp.bfloat16):
    array = scale * jax.random.normal(stream_key, extent, jnp.float32)
    if split:
        array = array * shard_levels(stream_key, extent, split, -0.22, 0.18)
    return jnp.clip(array, -bound, bound).astype(held_as)


def setup_inputs(seed: int = 0) -> dict:
    streams_of = jax.random.split(jax.random.key(seed), 8)
    return {
        "eigvectors": normal_values(streams_of[0], (N, M), (0.5 * N ** -0.25), 0.4375, ((0, 32), (1, 16))),
        "panel_vectors": normal_values(streams_of[1], (2, P_SIZE, N), ((P_SIZE * N) ** -0.25), 0.21875, ((1, 16), (2, 32))),
        "panel_factors": normal_values(streams_of[2], (2, P_SIZE, P_SIZE), P_SIZE ** -0.5, 0.375, (), jnp.float32),
        "eigenvalues": jnp.clip(jnp.exp(jax.random.uniform(streams_of[3], (M,), jnp.float32, math.log(4.0), math.log(400.0))), 4.0, 400.0),
        "damping": jnp.clip(jnp.exp(jax.random.uniform(streams_of[4], (M,), jnp.float32, math.log(0.02), math.log(0.1))), 0.02, 0.1),
        "frequencies": jnp.clip(jax.random.uniform(streams_of[5], (FREQ,), jnp.float32, 4.0, 16.0), 4.0, 16.0),
        "loads": normal_values(streams_of[6], (L, N), 1.0, 6.0, ((1, 512),)),
    }


def transfer(eigenvalues, damping, frequencies):
    detune = eigenvalues[None, :] - frequencies[:, None] * frequencies[:, None]
    width = 2.0 * damping[None, :] * frequencies[:, None] * jnp.sqrt(eigenvalues)[None, :]
    denom = detune * detune + width * width
    return (detune / denom, -width / denom)

def reference(eigvectors, panel_vectors, panel_factors, eigenvalues, damping, frequencies, loads):
    highest = lax.Precision.HIGHEST
    upper = jnp.triu(panel_factors)
    first = panel_vectors[0]
    second = panel_vectors[1]
    w_first = jnp.dot(first, eigvectors, preferred_element_type=jnp.float32)
    y_first = jnp.dot(upper[0].T, w_first, precision=highest).astype(jnp.bfloat16)
    z_first = eigvectors.astype(jnp.float32) - lax.dot_general(first, y_first, (((0,), (0,)), ((), ())), preferred_element_type=jnp.float32)
    w_second = jnp.dot(second.astype(jnp.float32), z_first, precision=highest)
    y_second = jnp.dot(upper[1].T, w_second, precision=highest).astype(jnp.bfloat16)
    rotated = (z_first - lax.dot_general(second, y_second, (((0,), (0,)), ((), ())), preferred_element_type=jnp.float32)).astype(jnp.bfloat16)
    modal = jnp.dot(loads, rotated, preferred_element_type=jnp.float32)
    h_real, h_imag = transfer(eigenvalues, damping, frequencies)

    def respond(pair):
        scaled_re = (modal * pair[0][None, :]).astype(jnp.bfloat16)
        scaled_im = (modal * pair[1][None, :]).astype(jnp.bfloat16)
        out_re = lax.dot_general(scaled_re, rotated, (((1,), (1,)), ((), ())), preferred_element_type=jnp.float32)
        out_im = lax.dot_general(scaled_im, rotated, (((1,), (1,)), ((), ())), preferred_element_type=jnp.float32)
        return (out_re.astype(jnp.bfloat16), out_im.astype(jnp.bfloat16))
    resp_real, resp_imag = lax.map(respond, (h_real, h_imag))
    return (resp_real, resp_imag)
```

```python
import jax
import jax.numpy as jnp
from jax import lax
from jax.sharding import PartitionSpec as P

HIGHEST = lax.Precision.HIGHEST


def transfer(eigenvalues, damping, frequencies):
    detune = eigenvalues[None, :] - frequencies[:, None] * frequencies[:, None]
    width = 2.0 * damping[None, :] * frequencies[:, None] * jnp.sqrt(eigenvalues)[None, :]
    denom = detune * detune + width * width
    return (detune / denom, -width / denom)


def exchange(chunks, axis):
    return lax.all_to_all(chunks, axis, split_axis=0, concat_axis=0, tiled=True)


def spread(value, axis, count):
    return exchange(jnp.broadcast_to(value[None], (count,) + value.shape), axis)


def dot32(left, right, dims):
    return lax.dot_general(left, right, (dims, ((), ())), preferred_element_type=jnp.float32)


def exact(left, right, dims):
    return lax.dot_general(left, right, (dims, ((), ())), precision=HIGHEST)


def body(eigvectors, panel_vectors, panel_factors, eigenvalues, damping, frequencies, loads):
    rows = lax.axis_size("row")
    cols = lax.axis_size("col")
    bf16 = jnp.bfloat16
    _, mine, dofs = panel_vectors.shape
    modes = eigvectors.shape[1]
    cases, block = loads.shape
    size = panel_factors.shape[-1]
    upper = jnp.triu(panel_factors)

    half = cases // 2
    folded = jnp.concatenate([loads[:half], loads[half:]], axis=1).reshape(2, mine, 2 * block)
    packed = jnp.concatenate([panel_vectors, folded], axis=2)
    gathered = lax.all_gather(packed, "col", axis=1, tiled=True)
    vectors = gathered[:, :, :dofs]

    cut = panel_vectors.reshape(2 * mine, cols, block).transpose(1, 0, 2)
    cut = exchange(cut, "col").reshape(cols, 2, mine, block).transpose(1, 0, 2, 3)
    cut = cut.reshape(2, size, block)
    last = ((1,), (1,))
    second_loads = jnp.concatenate([cut[1], loads], axis=0)
    gram = jnp.concatenate([dot32(second_loads, cut[0], last), dot32(loads, cut[1], last)], axis=0)
    wide = gram.shape[1] // 2
    gram = jnp.concatenate([gram[:, :wide], gram[:, wide:]], axis=0)
    piece = gram.shape[0] // rows
    gram = jnp.sum(exchange(gram.reshape(rows, piece, wide), "row"), axis=0)
    gram = jnp.sum(spread(gram, "col", cols), axis=0)

    tail = gathered[:, :, dofs:].reshape(2, cols, mine, 2, block)
    tail = tail.transpose(3, 0, 2, 1, 4).reshape(cases, dofs)
    panels = dot32(eigvectors, vectors, ((0,), (2,))).reshape(modes, 2 * size)
    direct = dot32(eigvectors, tail, ((0,), (1,)))
    part = jnp.concatenate([panels, direct], axis=1)
    width = part.shape[1]
    share = modes // rows
    part = part.reshape(rows, share * width)
    sent = jnp.concatenate([part, jnp.broadcast_to(gram.reshape(1, -1), (rows, piece * wide))], axis=1)
    got = exchange(sent.reshape(rows, -1, 128), "row").reshape(rows, -1)
    total = jnp.sum(got[:, : share * width].reshape(rows, share, width), axis=0)
    gram = got[:, share * width :].reshape(2, rows * piece // 2, wide)
    gram = jnp.concatenate([gram[0], gram[1]], axis=1)

    inner = ((1,), (0,))
    y_first = exact(total[:, :size], upper[0], inner).astype(bf16)
    first32 = y_first.astype(jnp.float32)
    other = total[:, size:] - exact(first32, gram[: size + cases], last)
    y_second = exact(other[:, :size], upper[1], inner).astype(bf16)
    modal = other[:, size:] - exact(y_second.astype(jnp.float32), gram[size + cases :], last)
    answer = jnp.concatenate([y_first, y_second, modal.astype(bf16)], axis=1)
    answer = spread(answer.reshape(-1, 128), "row", rows).reshape(modes, width)

    weights = answer[:, : 2 * size].reshape(modes, 2, size)
    applied = dot32(vectors, weights, ((0, 1), (1, 2)))
    rotated = (eigvectors.astype(jnp.float32) - applied).astype(bf16)
    own_modal = answer[:, 2 * size :].T
    sent = jnp.concatenate(
        [rotated.reshape(cols, block, modes), jnp.broadcast_to(own_modal[None], (cols, cases, modes))], axis=1
    )
    got = exchange(sent, "col")
    all_modes = got[:, :block]
    all_modal = got[:, block:].astype(jnp.float32)

    h_real, h_imag = transfer(eigenvalues, damping, frequencies)
    count = frequencies.shape[0]
    scale = jnp.stack([h_real, h_imag]).reshape(2, count, cols, 1, modes)
    scaled = (all_modal[None, None] * scale).astype(bf16)
    product = lax.dot_general(
        scaled, all_modes, (((2, 4), (0, 2)), ((), ())), preferred_element_type=jnp.float32
    ).astype(bf16)
    return (product[0], product[1])


def solution(mesh):
    return jax.shard_map(
        body,
        mesh=mesh,
        in_specs=(
            P("row", "col"),
            P(None, "col", "row"),
            P(),
            P(),
            P(),
            P(),
            P(None, ("row", "col")),
        ),
        out_specs=(P(None, None, ("row", "col")), P(None, None, ("row", "col"))),
        check_vma=False,
    )
```

```python
import jax
import jax.numpy as jnp
from jax import lax
from jax.experimental import pallas as pl
from jax.experimental.pallas import tpu as pltpu
from jax.sharding import Mesh
from jax.sharding import PartitionSpec as P

LINK = jnp.bfloat16
F32 = jnp.float32
VMEM_LIMIT = 24 * 2**20
COL = ("y", "core")
LAST = (((1,), (1,)), ((), ()))
OFFSETS = (0, -1, 1, -2, 2, -3, 3, -4)
SOON = 5
DEPTH = 768


def transfer(eigenvalues, damping, frequencies):
    detune = eigenvalues[None, :] - frequencies[:, None] * frequencies[:, None]
    width = 2.0 * damping[None, :] * frequencies[:, None] * jnp.sqrt(eigenvalues)[None, :]
    denom = detune * detune + width * width
    return (detune / denom, -width / denom)


def exchange(chunks, axis):
    return lax.all_to_all(chunks, axis, split_axis=0, concat_axis=0, tiled=True)


def spread(value, axis, count):
    return exchange(jnp.broadcast_to(value[None], (count,) + value.shape), axis)


def dot32(left, right):
    return jnp.dot(left, right, preferred_element_type=F32)


def outer32(left, right):
    return lax.dot_general(left, right, LAST, preferred_element_type=F32)


def panel(refs, index, lanes):
    parts = [ref[:, index, :, lanes] for ref in refs]
    return jnp.concatenate([p.reshape(p.shape[0] * p.shape[1], p.shape[2]) for p in parts], axis=0)


def factors_kernel(here_ref, factor_ref, out_ref):
    size = factor_ref.shape[1]
    count = len(OFFSETS)
    mine = size // (2 * count)
    core, place = here_ref[0], here_ref[1]
    square, strip = (size, size), (mine, size)
    keep = lax.broadcasted_iota(jnp.int32, square, 1) >= lax.broadcasted_iota(jnp.int32, square, 0)
    gap = lax.broadcasted_iota(jnp.int32, strip, 1) - lax.broadcasted_iota(jnp.int32, strip, 0)
    order = []
    for flip in (0, 1):
        for offset in OFFSETS:
            owner = 2 * lax.rem(place + offset + count, count) + (core if flip == 0 else 1 - core)
            order.append(jnp.where(gap == mine * owner, 1.0, 0.0))
    order = jnp.concatenate(order, axis=0).astype(jnp.bfloat16)
    for k in range(2):
        rest = jnp.where(keep, factor_ref[k], 0.0).T
        for part in range(2):
            piece = rest.astype(jnp.bfloat16)
            rest = rest - piece.astype(F32)
            out_ref[k, part] = outer32(dot32(order, piece).astype(jnp.bfloat16), order).astype(jnp.bfloat16)


def products_kernel(here_ref, *refs):
    shards, eig_ref, out_ref, tails, loads = refs[:4], refs[4], refs[5], refs[6], refs[7]
    core, place = here_ref[0], here_ref[1]
    count = len(OFFSETS)
    dofs, modes = eig_ref.shape
    cases = loads.shape[0]
    half = cases // 2
    block = dofs // (2 * count)
    behind = slice(dofs, dofs + 2 * block)
    for flip in (0, 1):
        near, far = shards[2 * flip : 2 * flip + 2]
        owner = core if flip == 0 else 1 - core
        for j, offset in enumerate(OFFSETS):
            value = near[j, :, :, behind] if j < near.shape[0] else far[j - near.shape[0], :, :, behind]
            tails[2 * lax.rem(place + offset + count, count) + owner] = value.reshape(half, 2 * block)
    for pair in range(count):
        even, odd = tails[2 * pair], tails[2 * pair + 1]
        at = slice(2 * pair * block, 2 * (pair + 1) * block)
        loads[:half, at] = jnp.concatenate([even[:, :block], odd[:, :block]], axis=1)
        loads[half:, at] = jnp.concatenate([even[:, block:], odd[:, block:]], axis=1)

    sums = cross = loaded = None
    for at in range(0, dofs, DEPTH):
        lanes = slice(at, at + DEPTH)
        first, second, case = panel(shards, 0, lanes), panel(shards, 1, lanes), loads[:, lanes]
        left = jnp.concatenate([first, second, case], axis=0)
        size = first.shape[0]
        new = dot32(left, eig_ref[lanes]), outer32(left[size:], first), outer32(case, second)
        sums, cross, loaded = new if at == 0 else (sums + new[0], cross + new[1], loaded + new[2])
    to = lambda value: value.astype(out_ref.dtype)
    rest = jnp.concatenate([cross[size:], loaded], axis=0)
    out_ref[:, :size] = to(cross[:size])
    out_ref[: size // 2, size : size + modes] = to(rest[:, :modes])
    out_ref[size // 2 :, size : size + modes] = to(rest[:, modes:])
    out_ref[:, size + modes : size + 2 * modes] = to(sums[:size])
    out_ref[:, size + 2 * modes : size + 3 * modes] = to(sums[size : 2 * size])
    out_ref[:cases, size + 3 * modes :] = to(sums[2 * size :])
    out_ref[cases:, size + 3 * modes :] = jnp.zeros((size - cases, modes), out_ref.dtype)


def rotate_kernel(total_ref, factor_ref, *refs):
    shards, eig_ref, out_ref = refs[:4], refs[4], refs[5]
    bf16 = jnp.bfloat16
    size = factor_ref.shape[2]
    dofs, modes = eig_ref.shape
    cases = size // 4
    block = out_ref.shape[1] - cases
    total = total_ref[...]
    rest = total[:, size : size + modes]
    rest = jnp.concatenate([rest[: size // 2], rest[size // 2 :]], axis=1)
    first = total[:, size + modes : size + 2 * modes]
    second = total[:, size + 2 * modes : size + 3 * modes].astype(F32)
    direct = total[:cases, size + 3 * modes :].astype(F32)
    first = (dot32(factor_ref[0, 0], first) + dot32(factor_ref[0, 1], first)).astype(bf16)
    second = second - dot32(total[:, :size], first)
    high = second.astype(bf16)
    low = (second - high.astype(F32)).astype(bf16)
    second = dot32(factor_ref[1, 0], high) + dot32(factor_ref[1, 1], high) + dot32(factor_ref[1, 0], low)
    second = second.astype(bf16)
    modal = (direct - dot32(rest[:cases], first) - dot32(rest[cases:], second)).astype(bf16)
    weights = jnp.concatenate([first, second], axis=0).T
    for at in range(0, dofs, DEPTH):
        lanes = slice(at, at + DEPTH)
        vectors = jnp.concatenate([panel(shards, 0, lanes), panel(shards, 1, lanes)], axis=0)
        rotated = (eig_ref[lanes].astype(F32) - dot32(weights, vectors).T).astype(bf16)
        for k in range(DEPTH // block):
            out_ref[at // block + k, :block] = rotated[k * block : (k + 1) * block]
            out_ref[at // block + k, block:] = modal


def gather_ring(packed, count):
    shift = [[(i, (i + s) % count) for i in range(count)] for s in (1, -1)]
    swap = [(0, 1), (1, 0)]
    held = [packed]
    up = down = packed
    for k in range(1, count // 2 + 1):
        up = lax.ppermute(up, "y", shift[0])
        held.append(up)
        if 2 * k < count:
            down = lax.ppermute(down, "y", shift[1])
            held.append(down)
    near, far = jnp.stack(held[:SOON]), jnp.stack(held[SOON:])
    return near, far, lax.ppermute(near, "core", swap), lax.ppermute(far, "core", swap)


def body(eigvectors, panel_vectors, panel_factors, eigenvalues, damping, frequencies, loads):
    rows = lax.axis_size("row")
    ys = lax.axis_size("y")
    cols = ys * 2
    bf16 = jnp.bfloat16
    _, mine, dofs = panel_vectors.shape
    modes = eigvectors.shape[1]
    cases, block = loads.shape
    size = panel_factors.shape[-1]
    width = size + 4 * modes
    here = jnp.stack([lax.axis_index("core"), lax.axis_index("y")])

    half = cases // 2
    folded = jnp.concatenate([loads[:half], loads[half:]], axis=1).reshape(2, mine, 2 * block)
    packed = jnp.concatenate([panel_vectors, folded], axis=2)
    shards = gather_ring(packed, ys)

    scalars = pl.BlockSpec(memory_space=pltpu.SMEM)
    vmem = pl.BlockSpec(memory_space=pltpu.VMEM)
    params = pltpu.CompilerParams(vmem_limit_bytes=VMEM_LIMIT)
    upper = pl.pallas_call(
        factors_kernel,
        in_specs=[scalars, vmem],
        out_specs=vmem,
        out_shape=jax.ShapeDtypeStruct((2, 2, size, size), bf16),
        compiler_params=params,
        cost_estimate=pl.CostEstimate(flops=16 * size**3, bytes_accessed=16 * size**2, transcendentals=0),
    )(here, panel_factors)
    sent = pl.pallas_call(
        products_kernel,
        in_specs=[scalars, vmem, vmem, vmem, vmem, vmem],
        out_specs=vmem,
        out_shape=jax.ShapeDtypeStruct((size, width), LINK),
        scratch_shapes=[pltpu.VMEM((cols, half, 2 * block), bf16), pltpu.VMEM((cases, dofs), bf16)],
        compiler_params=params,
    )(here, *shards, eigvectors)

    total = jnp.sum(exchange(sent.reshape(rows, size // rows, width), "row").astype(F32), axis=0)
    total = spread(total.astype(LINK), "row", rows).reshape(size, width)

    sent = pl.pallas_call(
        rotate_kernel,
        in_specs=[vmem] * 7,
        out_specs=vmem,
        out_shape=jax.ShapeDtypeStruct((cols, block + cases, modes), bf16),
        compiler_params=params,
    )(total, upper, *shards, eigvectors)
    got = exchange(sent, COL)
    all_modes = got[:, :block]
    all_modal = got[:, block:].astype(F32)

    h_real, h_imag = transfer(eigenvalues, damping, frequencies)
    count = frequencies.shape[0]
    scale = jnp.stack([h_real, h_imag]).reshape(2, count, cols, 1, modes)
    scaled = (all_modal[None, None] * scale).astype(bf16)
    product = lax.dot_general(
        scaled, all_modes, (((2, 4), (0, 2)), ((), ())), preferred_element_type=F32
    ).astype(bf16)
    return (product[0], product[1])


def solution(mesh):
    mesh = Mesh(mesh.devices.reshape(32, 8, 2), ("row", "y", "core"))
    everywhere = P(None, None, ("row", "y", "core"))
    return jax.shard_map(
        body,
        mesh=mesh,
        in_specs=(P("row", COL), P(None, COL, "row"), P(), P(), P(), P(), P(None, ("row", "y", "core"))),
        out_specs=(everywhere, everywhere),
        check_vma=False,
    )
```

```python
import jax
import jax.numpy as jnp
from jax import lax
from jax.experimental import pallas as pl
from jax.experimental.pallas import tpu as pltpu
from jax.sharding import Mesh
from jax.sharding import PartitionSpec as P

LINK = jnp.bfloat16
F32 = jnp.float32
VMEM_LIMIT = 24 * 2**20
COL = ("y", "core")
LAST = (((1,), (1,)), ((), ()))
OFFSETS = (0, -1, 1, -2, 2, -3, 3, -4)
DEPTH = 768
SOON = 5
SHARDS = 4


def transfer(eigenvalues, damping, frequencies):
    detune = eigenvalues[None, :] - frequencies[:, None] * frequencies[:, None]
    width = 2.0 * damping[None, :] * frequencies[:, None] * jnp.sqrt(eigenvalues)[None, :]
    denom = detune * detune + width * width
    return (detune / denom, -width / denom)


def exchange(chunks, axis):
    return lax.all_to_all(chunks, axis, split_axis=0, concat_axis=0, tiled=True)


def dot32(left, right):
    return jnp.dot(left, right, preferred_element_type=F32)


def outer32(left, right):
    return lax.dot_general(left, right, LAST, preferred_element_type=F32)


def panel(refs, index, lanes):
    parts = [ref[:, index, :, lanes] for ref in refs]
    return jnp.concatenate([p.reshape(p.shape[0] * p.shape[1], p.shape[2]) for p in parts], axis=0)


def pack_kernel(vectors_hbm, loads_hbm, out_ref, loads_ref, sems):
    dofs = vectors_hbm.shape[2]
    copies = [
        pltpu.make_async_copy(vectors_hbm, out_ref.at[:, :, :dofs], sems.at[0]),
        pltpu.make_async_copy(loads_hbm, loads_ref, sems.at[1]),
    ]
    for copy in copies:
        copy.start()
    copies[1].wait()
    half = loads_ref.shape[0] // 2
    folded = jnp.concatenate([loads_ref[:half], loads_ref[half:]], axis=1)
    out_ref[:, :, dofs:] = folded.reshape(out_ref.shape[0], out_ref.shape[1], folded.shape[1])
    copies[0].wait()


def sum_kernel(parts_ref, out_ref):
    total = jnp.sum(parts_ref[...].astype(F32), axis=0).astype(out_ref.dtype)
    out_ref[...] = jnp.broadcast_to(total[None], out_ref.shape)


def factors_kernel(here_ref, factor_ref, out_ref):
    size = factor_ref.shape[1]
    count = len(OFFSETS)
    mine = size // (2 * count)
    core, place = here_ref[0], here_ref[1]
    square, strip = (size, size), (mine, size)
    keep = lax.broadcasted_iota(jnp.int32, square, 1) >= lax.broadcasted_iota(jnp.int32, square, 0)
    gap = lax.broadcasted_iota(jnp.int32, strip, 1) - lax.broadcasted_iota(jnp.int32, strip, 0)
    order = []
    for flip in (0, 1):
        for offset in OFFSETS:
            owner = 2 * lax.rem(place + offset + count, count) + (core if flip == 0 else 1 - core)
            order.append(jnp.where(gap == mine * owner, 1.0, 0.0))
    order = jnp.concatenate(order, axis=0).astype(jnp.bfloat16)
    for k in range(2):
        rest = jnp.where(keep, factor_ref[k], 0.0).T
        for part in range(2):
            piece = rest.astype(jnp.bfloat16)
            rest = rest - piece.astype(F32)
            out_ref[k, part] = outer32(dot32(order, piece).astype(jnp.bfloat16), order).astype(jnp.bfloat16)


def products_kernel(here_ref, *refs):
    shards, eig_hbm, out_ref, (eig_ref, tails, loads, sem) = refs[:SHARDS], refs[SHARDS], refs[SHARDS + 1], refs[SHARDS + 2 :]
    copy = pltpu.make_async_copy(eig_hbm, eig_ref, sem)
    copy.start()
    core, place = here_ref[0], here_ref[1]
    count = len(OFFSETS)
    dofs, modes = eig_ref.shape
    cases = loads.shape[0]
    half = cases // 2
    block = dofs // (2 * count)
    behind = slice(dofs, dofs + 2 * block)
    blocks = [ref.at[j] for ref in shards for j in range(ref.shape[0])]
    for flip in (0, 1):
        owner = core if flip == 0 else 1 - core
        for j, offset in enumerate(OFFSETS):
            value = blocks[flip * count + j][:, :, behind]
            tails[2 * lax.rem(place + offset + count, count) + owner] = value.reshape(half, 2 * block)
    for pair in range(count):
        even, odd = tails[2 * pair], tails[2 * pair + 1]
        at = slice(2 * pair * block, 2 * (pair + 1) * block)
        loads[:half, at] = jnp.concatenate([even[:, :block], odd[:, :block]], axis=1)
        loads[half:, at] = jnp.concatenate([even[:, block:], odd[:, block:]], axis=1)

    size = out_ref.shape[0]
    cross = loaded = sums = None
    for at in range(0, dofs, DEPTH):
        lanes = slice(at, at + DEPTH)
        first, second, case = panel(shards, 0, lanes), panel(shards, 1, lanes), loads[:, lanes]
        new = outer32(jnp.concatenate([second, case], axis=0), first), outer32(case, second)
        cross, loaded = new if at == 0 else (cross + new[0], loaded + new[1])
        if at == 0:
            copy.wait()
        new = dot32(jnp.concatenate([first, second, case], axis=0), eig_ref[lanes])
        sums = new if at == 0 else sums + new
    to = lambda value: value.astype(out_ref.dtype)
    rest = jnp.concatenate([cross[size:], loaded], axis=0)
    out_ref[:, :size] = to(cross[:size])
    out_ref[: size // 2, size : size + modes] = to(rest[:, :modes])
    out_ref[size // 2 :, size : size + modes] = to(rest[:, modes:])
    out_ref[:, size + modes : size + 2 * modes] = to(sums[:size])
    out_ref[:, size + 2 * modes : size + 3 * modes] = to(sums[size : 2 * size])
    out_ref[:cases, size + 3 * modes :] = to(sums[2 * size :])
    out_ref[cases:, size + 3 * modes :] = jnp.zeros((size - cases, modes), out_ref.dtype)


def rotate_kernel(total_ref, factor_ref, *refs):
    shards, eig_hbm, out_hbm, (eig_ref, out_ref, eig_sem, out_sem) = refs[:SHARDS], refs[SHARDS], refs[SHARDS + 1], refs[SHARDS + 2 :]
    bf16 = jnp.bfloat16
    eig_copy = pltpu.make_async_copy(eig_hbm, eig_ref, eig_sem)
    eig_copy.start()
    size = factor_ref.shape[2]
    dofs, modes = eig_ref.shape
    cases = size // 4
    block = out_ref.shape[1] - cases
    total = total_ref[...]
    rest = total[:, size : size + modes]
    rest = jnp.concatenate([rest[: size // 2], rest[size // 2 :]], axis=1)
    first = total[:, size + modes : size + 2 * modes]
    second = total[:, size + 2 * modes : size + 3 * modes].astype(F32)
    direct = total[:cases, size + 3 * modes :].astype(F32)
    first = (dot32(factor_ref[0, 0], first) + dot32(factor_ref[0, 1], first)).astype(bf16)
    second = second - dot32(total[:, :size], first)
    high = second.astype(bf16)
    low = (second - high.astype(F32)).astype(bf16)
    second = dot32(factor_ref[1, 0], high) + dot32(factor_ref[1, 1], high) + dot32(factor_ref[1, 0], low)
    second = second.astype(bf16)
    modal = (direct - dot32(rest[:cases], first) - dot32(rest[cases:], second)).astype(bf16)
    weights = jnp.concatenate([first, second], axis=0).T
    eig_copy.wait()
    copies = []
    for at in range(0, dofs, DEPTH):
        lanes = slice(at, at + DEPTH)
        vectors = jnp.concatenate([panel(shards, 0, lanes), panel(shards, 1, lanes)], axis=0)
        rotated = (eig_ref[lanes].astype(F32) - dot32(weights, vectors).T).astype(bf16)
        for k in range(DEPTH // block):
            out_ref[at // block + k, :block] = rotated[k * block : (k + 1) * block]
            out_ref[at // block + k, block:] = modal
        ready = slice(at // block, (at + DEPTH) // block)
        copies.append(pltpu.make_async_copy(out_ref.at[ready], out_hbm.at[ready], out_sem.at[len(copies)]))
        copies[-1].start()
    for copy in copies:
        copy.wait()


def gather_ring(packed, count, upper):
    shift = [[(i, (i + s) % count) for i in range(count)] for s in (1, -1)]
    swap = lambda blocks: lax.ppermute(blocks, "core", [(0, 1), (1, 0)])
    held = [packed]
    up = down = packed
    for k in range(1, count // 2 + 1):
        up = lax.ppermute(up, "y", shift[0])
        held.append(up)
        if k == 2:
            up, upper = lax.optimization_barrier((up, upper))
        if 2 * k < count:
            down = lax.ppermute(down, "y", shift[1])
            held.append(down)
    near, far = jnp.stack(held[:SOON]), jnp.stack(held[SOON:])
    return (near, far, swap(near), swap(far)), upper


def body(eigvectors, panel_vectors, panel_factors, eigenvalues, damping, frequencies, loads):
    rows = lax.axis_size("row")
    ys = lax.axis_size("y")
    cols = ys * 2
    bf16 = jnp.bfloat16
    _, mine, dofs = panel_vectors.shape
    modes = eigvectors.shape[1]
    cases, block = loads.shape
    size = panel_factors.shape[-1]
    width = size + 4 * modes
    here = jnp.stack([lax.axis_index("core"), lax.axis_index("y")])

    scalars = pl.BlockSpec(memory_space=pltpu.SMEM)
    vmem = pl.BlockSpec(memory_space=pltpu.VMEM)
    hbm = pl.BlockSpec(memory_space=pl.ANY)
    params = pltpu.CompilerParams(vmem_limit_bytes=VMEM_LIMIT)
    upper = pl.pallas_call(
        factors_kernel,
        in_specs=[scalars, vmem],
        out_specs=vmem,
        out_shape=jax.ShapeDtypeStruct((2, 2, size, size), bf16),
        compiler_params=params,
        cost_estimate=pl.CostEstimate(flops=16 * size**3, bytes_accessed=16 * size**2, transcendentals=0),
    )(here, panel_factors)

    packed = pl.pallas_call(
        pack_kernel,
        in_specs=[hbm, hbm],
        out_specs=vmem,
        out_shape=jax.ShapeDtypeStruct((2, mine, dofs + 2 * block), bf16),
        scratch_shapes=[pltpu.VMEM(loads.shape, bf16), pltpu.SemaphoreType.DMA((2,))],
        compiler_params=pltpu.CompilerParams(vmem_limit_bytes=60 * 2**20),
    )(panel_vectors, loads)
    shards, upper = gather_ring(packed, ys, upper)
    sent = pl.pallas_call(
        products_kernel,
        in_specs=[scalars] + [vmem] * SHARDS + [hbm],
        out_specs=vmem,
        out_shape=jax.ShapeDtypeStruct((size, width), LINK),
        scratch_shapes=[
            pltpu.VMEM((dofs, modes), bf16),
            pltpu.VMEM((cols, cases // 2, 2 * block), bf16),
            pltpu.VMEM((cases, dofs), bf16),
            pltpu.SemaphoreType.DMA,
        ],
        compiler_params=params,
    )(here, *shards, eigvectors)

    parts = exchange(sent.reshape(rows, size // rows, width), "row")
    total = pl.pallas_call(
        sum_kernel,
        in_specs=[vmem],
        out_specs=vmem,
        out_shape=jax.ShapeDtypeStruct(parts.shape, LINK),
        compiler_params=params,
    )(parts)
    total = exchange(total, "row").reshape(size, width)

    sent = pl.pallas_call(
        rotate_kernel,
        in_specs=[vmem] * (2 + SHARDS) + [hbm],
        out_specs=hbm,
        out_shape=jax.ShapeDtypeStruct((cols, block + cases, modes), bf16),
        scratch_shapes=[
            pltpu.VMEM((dofs, modes), bf16),
            pltpu.VMEM((cols, block + cases, modes), bf16),
            pltpu.SemaphoreType.DMA,
            pltpu.SemaphoreType.DMA((dofs // DEPTH,)),
        ],
        compiler_params=params,
    )(total, upper, *shards, eigvectors)
    got = exchange(sent, COL)
    all_modes = got[:, :block]
    all_modal = got[:, block:].astype(F32)

    h_real, h_imag = transfer(eigenvalues, damping, frequencies)
    count = frequencies.shape[0]
    scale = jnp.stack([h_real, h_imag]).reshape(2, count, cols, 1, modes)
    scaled = (all_modal[None, None] * scale).astype(bf16)
    product = lax.dot_general(scaled, all_modes, (((2, 4), (0, 2)), ((), ())), preferred_element_type=F32)
    product = product.astype(bf16)
    return (product[0], product[1])


def solution(mesh):
    mesh = Mesh(mesh.devices.reshape(32, 8, 2), ("row", "y", "core"))
    everywhere = P(None, None, ("row", "y", "core"))
    return jax.shard_map(
        body,
        mesh=mesh,
        in_specs=(P("row", COL), P(None, COL, "row"), P(), P(), P(), P(), P(None, ("row", "y", "core"))),
        out_specs=(everywhere, everywhere),
        check_vma=False,
    )
```

```python
import jax
import jax.numpy as jnp
from jax import lax
from jax.experimental import pallas as pl
from jax.experimental.pallas import tpu as pltpu
from jax.sharding import Mesh
from jax.sharding import PartitionSpec as P

LINK = jnp.bfloat16
F32 = jnp.float32
VMEM_LIMIT = 24 * 2**20
COL = ("y", "core")
LAST = (((1,), (1,)), ((), ()))
OFFSETS = (0, -1, 1, -2, 2, -3, 3, -4)
DEPTH = 768
SOON = 5
SHARDS = 4


def transfer(eigenvalues, damping, frequencies):
    detune = eigenvalues[None, :] - frequencies[:, None] * frequencies[:, None]
    width = 2.0 * damping[None, :] * frequencies[:, None] * jnp.sqrt(eigenvalues)[None, :]
    denom = detune * detune + width * width
    return (detune / denom, -width / denom)


def exchange(chunks, axis):
    return lax.all_to_all(chunks, axis, split_axis=0, concat_axis=0, tiled=True)


def dot32(left, right):
    return jnp.dot(left, right, preferred_element_type=F32)


def outer32(left, right):
    return lax.dot_general(left, right, LAST, preferred_element_type=F32)


def panel(refs, index, lanes):
    parts = [ref[:, index, :, lanes] for ref in refs]
    return jnp.concatenate([p.reshape(p.shape[0] * p.shape[1], p.shape[2]) for p in parts], axis=0)


def pack_kernel(vectors_hbm, loads_hbm, out_ref, loads_ref, sems):
    dofs = vectors_hbm.shape[2]
    copies = [
        pltpu.make_async_copy(vectors_hbm, out_ref.at[:, :, :dofs], sems.at[0]),
        pltpu.make_async_copy(loads_hbm, loads_ref, sems.at[1]),
    ]
    for copy in copies:
        copy.start()
    copies[1].wait()
    half = loads_ref.shape[0] // 2
    folded = jnp.concatenate([loads_ref[:half], loads_ref[half:]], axis=1)
    out_ref[:, :, dofs:] = folded.reshape(out_ref.shape[0], out_ref.shape[1], folded.shape[1])
    copies[0].wait()


def sum_kernel(parts_ref, out_ref):
    total = jnp.sum(parts_ref[...].astype(F32), axis=0).astype(out_ref.dtype)
    out_ref[...] = jnp.broadcast_to(total[None], out_ref.shape)


def factors_kernel(here_ref, factor_ref, out_ref):
    size = factor_ref.shape[1]
    count = len(OFFSETS)
    mine = size // (2 * count)
    core, place = here_ref[0], here_ref[1]
    square, strip = (size, size), (mine, size)
    keep = lax.broadcasted_iota(jnp.int32, square, 1) >= lax.broadcasted_iota(jnp.int32, square, 0)
    gap = lax.broadcasted_iota(jnp.int32, strip, 1) - lax.broadcasted_iota(jnp.int32, strip, 0)
    order = []
    for flip in (0, 1):
        for offset in OFFSETS:
            owner = 2 * lax.rem(place + offset + count, count) + (core if flip == 0 else 1 - core)
            order.append(jnp.where(gap == mine * owner, 1.0, 0.0))
    order = jnp.concatenate(order, axis=0).astype(jnp.bfloat16)
    for k in range(2):
        rest = jnp.where(keep, factor_ref[k], 0.0).T
        for part in range(2):
            piece = rest.astype(jnp.bfloat16)
            rest = rest - piece.astype(F32)
            out_ref[k, part] = outer32(dot32(order, piece).astype(jnp.bfloat16), order).astype(jnp.bfloat16)


def products_kernel(here_ref, *refs):
    shards, eig_hbm, out_ref, (eig_ref, tails, loads, sem) = refs[:SHARDS], refs[SHARDS], refs[SHARDS + 1], refs[SHARDS + 2 :]
    copy = pltpu.make_async_copy(eig_hbm, eig_ref, sem)
    copy.start()
    core, place = here_ref[0], here_ref[1]
    count = len(OFFSETS)
    dofs, modes = eig_ref.shape
    cases = loads.shape[0]
    half = cases // 2
    block = dofs // (2 * count)
    behind = slice(dofs, dofs + 2 * block)
    blocks = [ref.at[j] for ref in shards for j in range(ref.shape[0])]
    for flip in (0, 1):
        owner = core if flip == 0 else 1 - core
        for j, offset in enumerate(OFFSETS):
            value = blocks[flip * count + j][:, :, behind]
            tails[2 * lax.rem(place + offset + count, count) + owner] = value.reshape(half, 2 * block)
    for pair in range(count):
        even, odd = tails[2 * pair], tails[2 * pair + 1]
        at = slice(2 * pair * block, 2 * (pair + 1) * block)
        loads[:half, at] = jnp.concatenate([even[:, :block], odd[:, :block]], axis=1)
        loads[half:, at] = jnp.concatenate([even[:, block:], odd[:, block:]], axis=1)

    size = out_ref.shape[0]
    cross = loaded = sums = None
    for at in range(0, dofs, DEPTH):
        lanes = slice(at, at + DEPTH)
        first, second, case = panel(shards, 0, lanes), panel(shards, 1, lanes), loads[:, lanes]
        own = size // 2
        new = outer32(jnp.concatenate([second, case], axis=0), first[:own]), outer32(case, second[:own])
        cross, loaded = new if at == 0 else (cross + new[0], loaded + new[1])
        if at == 0:
            copy.wait()
        new = dot32(jnp.concatenate([first, second, case], axis=0), eig_ref[lanes])
        sums = new if at == 0 else sums + new
    rest = jnp.concatenate([cross[size:], loaded], axis=0)
    columns = [
        cross[:size],
        sums[:size],
        sums[size : 2 * size],
        fold(rest, 2),
        fold(sums[2 * size :], 4),
        jnp.zeros((size, modes // 4), F32),
    ]
    start = 0
    for column in columns:
        out_ref[:, start : start + column.shape[1]] = column.astype(out_ref.dtype)
        start += column.shape[1]


def fold(value, count):
    width = value.shape[1] // count
    return jnp.concatenate([value[:, k * width : (k + 1) * width] for k in range(count)], axis=0)


def unfold(value, count):
    height = value.shape[0] // count
    return jnp.concatenate([value[k * height : (k + 1) * height] for k in range(count)], axis=1)


def first_kernel(total_ref, factor_ref, *refs):
    shards, (weights_ref, partial_ref, applied_ref) = refs[:SHARDS], refs[SHARDS:]
    modes = applied_ref.shape[0]
    size = factor_ref.shape[2]
    dofs = applied_ref.shape[1]
    own = size // 2
    sums = total_ref[:, modes : 2 * modes]
    first = (dot32(factor_ref[0, 0], sums) + dot32(factor_ref[0, 1], sums)).astype(jnp.bfloat16)
    weights_ref[...] = first
    partial_ref[:size] = dot32(total_ref[:, :own], first[:own])
    rest = unfold(total_ref[:, 3 * modes : 3 * modes + modes // 2], 2)
    partial_ref[size:] = dot32(rest[: own // 2], first[:own])
    turned = first.T
    for at in range(0, dofs, DEPTH):
        lanes = slice(at, at + DEPTH)
        applied_ref[:, lanes] = dot32(turned, panel(shards, 0, lanes))


def second_kernel(total_ref, other_ref, weights_ref, partial_ref, applied_ref, factor_ref, *refs):
    shards, eig_hbm, out_hbm, (eig_ref, out_ref, eig_sem, out_sem) = refs[:SHARDS], refs[SHARDS], refs[SHARDS + 1], refs[SHARDS + 2 :]
    bf16 = jnp.bfloat16
    eig_copy = pltpu.make_async_copy(eig_hbm, eig_ref, eig_sem)
    eig_copy.start()
    size = factor_ref.shape[2]
    dofs, modes = eig_ref.shape
    cases = size // 4
    own = size // 2
    block = out_ref.shape[1] - cases
    ends = slice(3 * modes, 3 * modes + modes // 2)
    here, there = unfold(total_ref[:, ends], 2), unfold(other_ref[:, ends], 2)
    direct = unfold(total_ref[:, ends.stop : ends.stop + modes // 4], 4).astype(F32)
    first = weights_ref[own:]
    cross = jnp.concatenate([other_ref[own:, :own], other_ref[:own, :own]], axis=0)
    second = total_ref[:, 2 * modes : 3 * modes].astype(F32) - partial_ref[:size] - dot32(cross, first)
    modal = direct - partial_ref[size:] - dot32(there[:cases], first)
    high = second.astype(bf16)
    low = (second - high.astype(F32)).astype(bf16)
    second = dot32(factor_ref[1, 0], high) + dot32(factor_ref[1, 1], high) + dot32(factor_ref[1, 0], low)
    second = second.astype(bf16)
    modal = (modal - dot32(here[cases:], second[:own]) - dot32(there[cases:], second[own:])).astype(bf16)
    turned = second.T
    eig_copy.wait()
    copies = []
    for at in range(0, dofs, DEPTH):
        lanes = slice(at, at + DEPTH)
        applied = applied_ref[:, lanes] + dot32(turned, panel(shards, 1, lanes))
        rotated = (eig_ref[lanes].astype(F32) - applied.T).astype(bf16)
        for k in range(DEPTH // block):
            out_ref[at // block + k, :block] = rotated[k * block : (k + 1) * block]
            out_ref[at // block + k, block:] = modal
        ready = slice(at // block, (at + DEPTH) // block)
        copies.append(pltpu.make_async_copy(out_ref.at[ready], out_hbm.at[ready], out_sem.at[len(copies)]))
        copies[-1].start()
    for copy in copies:
        copy.wait()


def gather_ring(packed, count, upper):
    shift = [[(i, (i + s) % count) for i in range(count)] for s in (1, -1)]
    swap = lambda blocks: lax.ppermute(blocks, "core", [(0, 1), (1, 0)])
    held = [packed]
    up = down = packed
    for k in range(1, count // 2 + 1):
        up = lax.ppermute(up, "y", shift[0])
        held.append(up)
        if k == 2:
            up, upper = lax.optimization_barrier((up, upper))
        if 2 * k < count:
            down = lax.ppermute(down, "y", shift[1])
            held.append(down)
    near, far = jnp.stack(held[:SOON]), jnp.stack(held[SOON:])
    return (near, far, swap(near), swap(far)), upper


def body(eigvectors, panel_vectors, panel_factors, eigenvalues, damping, frequencies, loads):
    rows = lax.axis_size("row")
    ys = lax.axis_size("y")
    cols = ys * 2
    bf16 = jnp.bfloat16
    _, mine, dofs = panel_vectors.shape
    modes = eigvectors.shape[1]
    cases, block = loads.shape
    size = panel_factors.shape[-1]
    width = 4 * modes
    here = jnp.stack([lax.axis_index("core"), lax.axis_index("y")])

    scalars = pl.BlockSpec(memory_space=pltpu.SMEM)
    vmem = pl.BlockSpec(memory_space=pltpu.VMEM)
    hbm = pl.BlockSpec(memory_space=pl.ANY)
    params = pltpu.CompilerParams(vmem_limit_bytes=VMEM_LIMIT)
    upper = pl.pallas_call(
        factors_kernel,
        in_specs=[scalars, vmem],
        out_specs=vmem,
        out_shape=jax.ShapeDtypeStruct((2, 2, size, size), bf16),
        compiler_params=params,
        cost_estimate=pl.CostEstimate(flops=16 * size**3, bytes_accessed=16 * size**2, transcendentals=0),
    )(here, panel_factors)

    packed = pl.pallas_call(
        pack_kernel,
        in_specs=[hbm, hbm],
        out_specs=vmem,
        out_shape=jax.ShapeDtypeStruct((2, mine, dofs + 2 * block), bf16),
        scratch_shapes=[pltpu.VMEM(loads.shape, bf16), pltpu.SemaphoreType.DMA((2,))],
        compiler_params=pltpu.CompilerParams(vmem_limit_bytes=60 * 2**20),
    )(panel_vectors, loads)
    shards, upper = gather_ring(packed, ys, upper)
    sent = pl.pallas_call(
        products_kernel,
        in_specs=[scalars] + [vmem] * SHARDS + [hbm],
        out_specs=vmem,
        out_shape=jax.ShapeDtypeStruct((size, width), LINK),
        scratch_shapes=[
            pltpu.VMEM((dofs, modes), bf16),
            pltpu.VMEM((cols, cases // 2, 2 * block), bf16),
            pltpu.VMEM((cases, dofs), bf16),
            pltpu.SemaphoreType.DMA,
        ],
        compiler_params=params,
    )(here, *shards, eigvectors)

    parts = exchange(sent.reshape(rows, size // rows, width), "row")
    total = pl.pallas_call(
        sum_kernel,
        in_specs=[vmem],
        out_specs=vmem,
        out_shape=jax.ShapeDtypeStruct(parts.shape, LINK),
        compiler_params=params,
    )(parts)
    total = exchange(total, "row").reshape(size, width)

    other = lax.ppermute(total, "core", [(0, 1), (1, 0)])
    begun = pl.pallas_call(
        first_kernel,
        in_specs=[vmem] * (2 + SHARDS),
        out_specs=[vmem] * 3,
        out_shape=[
            jax.ShapeDtypeStruct((size, modes), bf16),
            jax.ShapeDtypeStruct((size + cases, modes), F32),
            jax.ShapeDtypeStruct((modes, dofs), F32),
        ],
        compiler_params=params,
        cost_estimate=pl.CostEstimate(flops=2 * size * modes * dofs, bytes_accessed=8 * 2**20, transcendentals=0),
    )(total, upper, *shards)
    sent = pl.pallas_call(
        second_kernel,
        in_specs=[vmem] * (6 + SHARDS) + [hbm],
        out_specs=hbm,
        out_shape=jax.ShapeDtypeStruct((cols, block + cases, modes), bf16),
        scratch_shapes=[
            pltpu.VMEM((dofs, modes), bf16),
            pltpu.VMEM((cols, block + cases, modes), bf16),
            pltpu.SemaphoreType.DMA,
            pltpu.SemaphoreType.DMA((dofs // DEPTH,)),
        ],
        compiler_params=params,
    )(total, other, *begun, upper, *shards, eigvectors)
    got = exchange(sent, COL)
    all_modes = got[:, :block]
    all_modal = got[:, block:].astype(F32)

    h_real, h_imag = transfer(eigenvalues, damping, frequencies)
    count = frequencies.shape[0]
    scale = jnp.stack([h_real, h_imag]).reshape(2, count, cols, 1, modes)
    scaled = (all_modal[None, None] * scale).astype(bf16)
    product = lax.dot_general(scaled, all_modes, (((2, 4), (0, 2)), ((), ())), preferred_element_type=F32)
    product = product.astype(bf16)
    return (product[0], product[1])


def solution(mesh):
    mesh = Mesh(mesh.devices.reshape(32, 8, 2), ("row", "y", "core"))
    everywhere = P(None, None, ("row", "y", "core"))
    return jax.shard_map(
        body,
        mesh=mesh,
        in_specs=(P("row", COL), P(None, COL, "row"), P(), P(), P(), P(), P(None, ("row", "y", "core"))),
        out_specs=(everywhere, everywhere),
        check_vma=False,
    )
```

```python
import jax
import jax.numpy as jnp
from jax import lax
from jax.experimental import pallas as pl
from jax.experimental.pallas import tpu as pltpu
from jax.sharding import Mesh
from jax.sharding import PartitionSpec as P

LINK = jnp.bfloat16
F32 = jnp.float32
VMEM_LIMIT = 24 * 2**20
COL = ("y", "core")
LAST = (((1,), (1,)), ((), ()))
OFFSETS = (0, -1, 1, -2, 2, -3, 3, -4)
DEPTH = 768
SOON = 5
SHARDS = 4


def transfer(eigenvalues, damping, frequencies):
    detune = eigenvalues[None, :] - frequencies[:, None] * frequencies[:, None]
    width = 2.0 * damping[None, :] * frequencies[:, None] * jnp.sqrt(eigenvalues)[None, :]
    denom = detune * detune + width * width
    return (detune / denom, -width / denom)


def exchange(chunks, axis):
    return lax.all_to_all(chunks, axis, split_axis=0, concat_axis=0, tiled=True)


def dot32(left, right):
    return jnp.dot(left, right, preferred_element_type=F32)


def outer32(left, right):
    return lax.dot_general(left, right, LAST, preferred_element_type=F32)


def panel(refs, index, lanes):
    parts = [ref[:, index, :, lanes] for ref in refs]
    return jnp.concatenate([p.reshape(p.shape[0] * p.shape[1], p.shape[2]) for p in parts], axis=0)


def pack_kernel(vectors_hbm, loads_hbm, out_ref, loads_ref, sems):
    dofs = vectors_hbm.shape[2]
    copies = [
        pltpu.make_async_copy(vectors_hbm, out_ref.at[:, :, :dofs], sems.at[0]),
        pltpu.make_async_copy(loads_hbm, loads_ref, sems.at[1]),
    ]
    for copy in copies:
        copy.start()
    copies[1].wait()
    half = loads_ref.shape[0] // 2
    folded = jnp.concatenate([loads_ref[:half], loads_ref[half:]], axis=1)
    out_ref[:, :, dofs:] = folded.reshape(out_ref.shape[0], out_ref.shape[1], folded.shape[1])
    copies[0].wait()


def sum_kernel(parts_ref, out_ref):
    total = jnp.sum(parts_ref[...].astype(F32), axis=0).astype(out_ref.dtype)
    out_ref[...] = jnp.broadcast_to(total[None], out_ref.shape)


def factors_kernel(here_ref, factor_ref, out_ref):
    size = factor_ref.shape[1]
    count = len(OFFSETS)
    mine = size // (2 * count)
    core, place = here_ref[0], here_ref[1]
    square, strip = (size, size), (mine, size)
    keep = lax.broadcasted_iota(jnp.int32, square, 1) >= lax.broadcasted_iota(jnp.int32, square, 0)
    gap = lax.broadcasted_iota(jnp.int32, strip, 1) - lax.broadcasted_iota(jnp.int32, strip, 0)
    order = []
    for flip in (0, 1):
        for offset in OFFSETS:
            owner = 2 * lax.rem(place + offset + count, count) + (core if flip == 0 else 1 - core)
            order.append(jnp.where(gap == mine * owner, 1.0, 0.0))
    order = jnp.concatenate(order, axis=0).astype(jnp.bfloat16)
    for k in range(2):
        rest = jnp.where(keep, factor_ref[k], 0.0).T
        for part in range(2):
            piece = rest.astype(jnp.bfloat16)
            rest = rest - piece.astype(F32)
            out_ref[k, part] = outer32(dot32(order, piece).astype(jnp.bfloat16), order).astype(jnp.bfloat16)


def place_loads(here_ref, shards, flip, tails, loads):
    core, place = here_ref[0], here_ref[1]
    count = len(OFFSETS)
    cases, dofs = loads.shape
    half, block = cases // 2, dofs // (2 * count)
    blocks = [ref.at[j] for ref in shards for j in range(ref.shape[0])]
    for j, offset in enumerate(OFFSETS):
        tails[lax.rem(place + offset + count, count)] = blocks[j][:, :, dofs : dofs + 2 * block].reshape(half, 2 * block)
    even = core == flip
    for pair in range(count):
        value = tails[pair]
        left, right = jnp.where(even, value, 0), jnp.where(even, 0, value)
        at = slice(2 * pair * block, 2 * (pair + 1) * block)
        loads[:half, at] = jnp.concatenate([left[:, :block], right[:, :block]], axis=1)
        loads[half:, at] = jnp.concatenate([left[:, block:], right[:, block:]], axis=1)


def accumulate(own, shards, loads, eig_ref, copy):
    gram = sums = None
    for at in range(0, eig_ref.shape[0], DEPTH):
        lanes = slice(at, at + DEPTH)
        first, second, case = panel(shards, 0, lanes), panel(shards, 1, lanes), loads[:, lanes]
        mine = (first, second) if own is shards else (panel(own, 0, lanes), panel(own, 1, lanes))
        left = jnp.concatenate([second, case], axis=0)
        new = jnp.concatenate([outer32(left, mine[0]), outer32(case, mine[1])], axis=0)
        gram = new if at == 0 else gram + new
        if at == 0 and copy is not None:
            copy.wait()
        new = dot32(jnp.concatenate([first, left], axis=0), eig_ref[lanes])
        sums = new if at == 0 else sums + new
    return sums, gram


def own_kernel(here_ref, near, far, eig_hbm, sums_ref, gram_ref, eig_ref, tails, loads, sem):
    copy = pltpu.make_async_copy(eig_hbm, eig_ref, sem)
    copy.start()
    shards = (near, far)
    place_loads(here_ref, shards, 0, tails, loads)
    sums_ref[...], gram_ref[...] = accumulate(shards, shards, loads, eig_ref, copy)


def other_kernel(here_ref, near, far, other_near, other_far, sums_ref, gram_ref, eig_ref, out_ref, tails, loads):
    shards = (other_near, other_far)
    place_loads(here_ref, shards, 1, tails, loads)
    sums, gram = accumulate((near, far), shards, loads, eig_ref, None)
    size, modes = out_ref.shape[0], eig_ref.shape[1]
    own = size // 2
    to = lambda value: value.astype(out_ref.dtype)
    out_ref[:own, :own] = to(gram_ref[:own])
    out_ref[own:, :own] = to(gram[:own])
    for k in range(2):
        at = slice(own + k * modes, own + (k + 1) * modes)
        out_ref[:own, at] = to(sums_ref[k * own : (k + 1) * own])
        out_ref[own:, at] = to(sums[k * own : (k + 1) * own])
    start = own + 2 * modes
    for value, count in ((gram_ref[own:] + gram[own:], 2), (sums_ref[size:] + sums[size:], 4)):
        value = fold(value, count)
        out_ref[:, start : start + value.shape[1]] = to(value)
        start += value.shape[1]
    out_ref[:, start:] = jnp.zeros((size, out_ref.shape[1] - start), out_ref.dtype)


def fold(value, count):
    width = value.shape[1] // count
    return jnp.concatenate([value[:, k * width : (k + 1) * width] for k in range(count)], axis=0)


def unfold(value, count):
    height = value.shape[0] // count
    return jnp.concatenate([value[k * height : (k + 1) * height] for k in range(count)], axis=1)


def first_kernel(total_ref, factor_ref, *refs):
    shards, (weights_ref, partial_ref, applied_ref) = refs[:SHARDS], refs[SHARDS:]
    modes = applied_ref.shape[0]
    size = factor_ref.shape[2]
    dofs = applied_ref.shape[1]
    own = size // 2
    sums = total_ref[:, modes : 2 * modes]
    first = (dot32(factor_ref[0, 0], sums) + dot32(factor_ref[0, 1], sums)).astype(jnp.bfloat16)
    weights_ref[...] = first
    partial_ref[:size] = dot32(total_ref[:, :own], first[:own])
    rest = unfold(total_ref[:, 3 * modes : 3 * modes + modes // 2], 2)
    partial_ref[size:] = dot32(rest[: own // 2], first[:own])
    turned = first.T
    for at in range(0, dofs, DEPTH):
        lanes = slice(at, at + DEPTH)
        applied_ref[:, lanes] = dot32(turned, panel(shards, 0, lanes))


def second_kernel(total_ref, other_ref, weights_ref, partial_ref, applied_ref, factor_ref, *refs):
    shards, eig_ref, out_hbm, (out_ref, out_sem) = refs[:SHARDS], refs[SHARDS], refs[SHARDS + 1], refs[SHARDS + 2 :]
    bf16 = jnp.bfloat16
    size = factor_ref.shape[2]
    dofs, modes = eig_ref.shape
    cases = size // 4
    own = size // 2
    block = out_ref.shape[1] - cases
    ends = slice(3 * modes, 3 * modes + modes // 2)
    here, there = unfold(total_ref[:, ends], 2), unfold(other_ref[:, ends], 2)
    direct = unfold(total_ref[:, ends.stop : ends.stop + modes // 4], 4).astype(F32)
    first = weights_ref[own:]
    cross = jnp.concatenate([other_ref[own:, :own], other_ref[:own, :own]], axis=0)
    second = total_ref[:, 2 * modes : 3 * modes].astype(F32) - partial_ref[:size] - dot32(cross, first)
    modal = direct - partial_ref[size:] - dot32(there[:cases], first)
    high = second.astype(bf16)
    low = (second - high.astype(F32)).astype(bf16)
    second = dot32(factor_ref[1, 0], high) + dot32(factor_ref[1, 1], high) + dot32(factor_ref[1, 0], low)
    second = second.astype(bf16)
    modal = (modal - dot32(here[cases:], second[:own]) - dot32(there[cases:], second[own:])).astype(bf16)
    turned = second.T
    copies = []
    for at in range(0, dofs, DEPTH):
        lanes = slice(at, at + DEPTH)
        applied = applied_ref[:, lanes] + dot32(turned, panel(shards, 1, lanes))
        rotated = (eig_ref[lanes].astype(F32) - applied.T).astype(bf16)
        for k in range(DEPTH // block):
            out_ref[at // block + k, :block] = rotated[k * block : (k + 1) * block]
            out_ref[at // block + k, block:] = modal
        ready = slice(at // block, (at + DEPTH) // block)
        copies.append(pltpu.make_async_copy(out_ref.at[ready], out_hbm.at[ready], out_sem.at[len(copies)]))
        copies[-1].start()
    for copy in copies:
        copy.wait()


def gather_ring(packed, count, upper):
    shift = [[(i, (i + s) % count) for i in range(count)] for s in (1, -1)]
    swap = lambda blocks: lax.ppermute(blocks, "core", [(0, 1), (1, 0)])
    held = [packed]
    up = down = packed
    for k in range(1, count // 2 + 1):
        up = lax.ppermute(up, "y", shift[0])
        held.append(up)
        if k == 2:
            up, upper = lax.optimization_barrier((up, upper))
        if 2 * k < count:
            down = lax.ppermute(down, "y", shift[1])
            held.append(down)
    near, far = jnp.stack(held[:SOON]), jnp.stack(held[SOON:])
    return (near, far, swap(near), swap(far)), upper


def body(eigvectors, panel_vectors, panel_factors, eigenvalues, damping, frequencies, loads):
    rows = lax.axis_size("row")
    ys = lax.axis_size("y")
    cols = ys * 2
    bf16 = jnp.bfloat16
    _, mine, dofs = panel_vectors.shape
    modes = eigvectors.shape[1]
    cases, block = loads.shape
    size = panel_factors.shape[-1]
    width = 4 * modes
    here = jnp.stack([lax.axis_index("core"), lax.axis_index("y")])

    scalars = pl.BlockSpec(memory_space=pltpu.SMEM)
    vmem = pl.BlockSpec(memory_space=pltpu.VMEM)
    hbm = pl.BlockSpec(memory_space=pl.ANY)
    far_memory = pl.BlockSpec(memory_space=pltpu.HBM)
    params = pltpu.CompilerParams(vmem_limit_bytes=VMEM_LIMIT)
    upper = pl.pallas_call(
        factors_kernel,
        in_specs=[scalars, vmem],
        out_specs=vmem,
        out_shape=jax.ShapeDtypeStruct((2, 2, size, size), bf16),
        compiler_params=params,
        cost_estimate=pl.CostEstimate(flops=16 * size**3, bytes_accessed=16 * size**2, transcendentals=0),
    )(here, panel_factors)

    packed = pl.pallas_call(
        pack_kernel,
        in_specs=[far_memory, far_memory],
        out_specs=vmem,
        out_shape=jax.ShapeDtypeStruct((2, mine, dofs + 2 * block), bf16),
        scratch_shapes=[pltpu.VMEM(loads.shape, bf16), pltpu.SemaphoreType.DMA((2,))],
        compiler_params=params,
    )(panel_vectors, loads)
    shards, upper = gather_ring(packed, ys, upper)
    own = size // 2
    scratch = [
        pltpu.VMEM((ys, cases // 2, 2 * block), bf16),
        pltpu.VMEM((cases, dofs), bf16),
    ]
    begun = pl.pallas_call(
        own_kernel,
        in_specs=[scalars, vmem, vmem, hbm],
        out_specs=[vmem] * 3,
        out_shape=[
            jax.ShapeDtypeStruct((size + cases, modes), F32),
            jax.ShapeDtypeStruct((own + 2 * cases, own), F32),
            jax.ShapeDtypeStruct(eigvectors.shape, bf16),
        ],
        scratch_shapes=[*scratch, pltpu.SemaphoreType.DMA],
        compiler_params=params,
        cost_estimate=pl.CostEstimate(flops=4 * size * modes * dofs, bytes_accessed=4 * 2**20, transcendentals=0),
    )(here, *shards[:2], eigvectors)
    sent = pl.pallas_call(
        other_kernel,
        in_specs=[scalars] + [vmem] * (SHARDS + 3),
        out_specs=vmem,
        out_shape=jax.ShapeDtypeStruct((size, width), LINK),
        scratch_shapes=scratch,
        compiler_params=params,
    )(here, *shards, *begun)
    eigvectors = begun[2]

    parts = exchange(sent.reshape(rows, size // rows, width), "row")
    total = pl.pallas_call(
        sum_kernel,
        in_specs=[vmem],
        out_specs=vmem,
        out_shape=jax.ShapeDtypeStruct(parts.shape, LINK),
        compiler_params=params,
    )(parts)
    total = exchange(total, "row").reshape(size, width)

    other = lax.ppermute(total, "core", [(0, 1), (1, 0)])
    begun = pl.pallas_call(
        first_kernel,
        in_specs=[vmem] * (2 + SHARDS),
        out_specs=[vmem] * 3,
        out_shape=[
            jax.ShapeDtypeStruct((size, modes), bf16),
            jax.ShapeDtypeStruct((size + cases, modes), F32),
            jax.ShapeDtypeStruct((modes, dofs), F32),
        ],
        compiler_params=params,
        cost_estimate=pl.CostEstimate(flops=2 * size * modes * dofs, bytes_accessed=8 * 2**20, transcendentals=0),
    )(total, upper, *shards)
    sent = pl.pallas_call(
        second_kernel,
        in_specs=[vmem] * (7 + SHARDS),
        out_specs=hbm,
        out_shape=jax.ShapeDtypeStruct((cols, block + cases, modes), bf16),
        scratch_shapes=[
            pltpu.VMEM((cols, block + cases, modes), bf16),
            pltpu.SemaphoreType.DMA((dofs // DEPTH,)),
        ],
        compiler_params=params,
    )(total, other, *begun, upper, *shards, eigvectors)
    got = exchange(sent, COL)
    all_modes = got[:, :block]
    all_modal = got[:, block:].astype(F32)

    h_real, h_imag = transfer(eigenvalues, damping, frequencies)
    count = frequencies.shape[0]
    scale = jnp.stack([h_real, h_imag]).reshape(2, count, cols, 1, modes)
    scaled = (all_modal[None, None] * scale).astype(bf16)
    product = lax.dot_general(scaled, all_modes, (((2, 4), (0, 2)), ((), ())), preferred_element_type=F32)
    product = product.astype(bf16)
    return (product[0], product[1])


def solution(mesh):
    mesh = Mesh(mesh.devices.reshape(32, 8, 2), ("row", "y", "core"))
    everywhere = P(None, None, ("row", "y", "core"))
    return jax.shard_map(
        body,
        mesh=mesh,
        in_specs=(P("row", COL), P(None, COL, "row"), P(), P(), P(), P(), P(None, ("row", "y", "core"))),
        out_specs=(everywhere, everywhere),
        check_vma=False,
    )
```
